32 devices in a mesh: grp: 2 (over y), row: 4 (over z), col: 2 (over x), sub: 2 (over core).
Axes of the slice: x: 2, y: 2, z: 4, core: 2. Of those that a mesh axis runs over, the one named last changes fastest.
Arguments:
- filament_slot: int32 [16384], P(('grp', 'row', 'col', 'sub')), parts along dimension 0, may hold values from 0 to 8191, each once
- wire_radius: float32 [16384], P(('grp', 'row', 'col', 'sub')), parts along dimension 0, may hold values from 0.02 to 0.05
- strand_radius: float32 [128], P('grp'), parts along dimension 0, may hold values from 0.2 to 1
- test_matrix: float32 [64, 16384], P(None, ('grp', 'row', 'col', 'sub')), parts along dimension 1, may hold values from -6 to 6
Outputs:
- ortho_basis: float32 [64, 16384], P(None, ('grp', 'row', 'col', 'sub')), parts along dimension 1
- sketch_factor: float32 [128, 64], P('grp'), parts along dimension 0
The draws below stay inside these ranges and needn't reach their ends.
There are 2 independent parts, one for each index of `grp`. The reference program is written for one: setup_inputs(seed, part) draws one part's arguments, and reference() takes and returns one part's arrays. A program takes and returns all parts, laid end to end along the dimension named above; each array names one. Nothing has to cross between parts.
Inputs may be any that keep to these rules, and one draw needn't show every extreme that they name: `filament_slot`: every number from 0 to 8191 occurs exactly once.
All inputs are finite; a program needn't handle non-finite values.
Results may differ from the reference program's by a relative error of at most 0.0005.
Values sent between devices are 32-bit elements; how exact they have to be, the bound alone decides.
A program may use at most 64 MiB of HBM per device.

```python
import math
import jax
import jax.numpy as jnp
from jax import lax

RANK = 64
SEGMENTS = 128
FILAMENTS = 8192
STRANDS = 64


def level_of(key, dims, cuts, low, high):
    loudness, own = 1.0, jax.random.fold_in(key, 6)
    for dim, parts in cuts:
        heights = jnp.exp(jax.random.uniform(jax.random.fold_in(own, dim), (parts,), jnp.float32, low / len(cuts), high / len(cuts)))
        loudness = loudness * jnp.repeat(heights, dims[dim] // parts).reshape([-1 if axis == dim else 1 for axis in range(len(dims))])
    return loudness


def centred(stream_key, dims, spread, most, split=(), kind=jnp.bfloat16):
    drawn = spread * jax.random.normal(stream_key, dims, jnp.float32)
    if split:
        drawn = drawn * level_of(stream_key, dims, split, -0.22, 0.18)
    return jnp.clip(drawn, -most, most).astype(kind)


def setup_inputs(seed: int = 0, part: int = 0) -> dict:
    arg_keys = jax.random.split(jax.random.key(seed), 5)
    own_keys = jax.random.split(jax.random.fold_in(arg_keys[4], part), 5)
    return {
        "filament_slot": jax.random.permutation(own_keys[0], FILAMENTS).astype(jnp.int32),
        "wire_radius": jnp.clip(0.02 + 0.030000001 * jax.random.uniform(own_keys[1], (FILAMENTS,), jnp.float32) ** level_of(own_keys[1], (FILAMENTS,), ((0, 16),), -0.2, 0.2), 0.02, 0.05),
        "strand_radius": jnp.clip(jax.random.uniform(own_keys[2], (STRANDS,), jnp.float32, 0.2, 1.0), 0.2, 1.0),
        "test_matrix": centred(own_keys[3], (RANK, FILAMENTS), 1.0, 6.0, ((1, 16),), jnp.float32),
    }


mu_scale = 1e-05
twist_rate = 4.0 * math.pi

def source_block(targets, sources, columns):
    delta_x = sources[0][:, None] - targets[0][None, :]
    delta_y = sources[1][:, None] - targets[1][None, :]
    delta_z = sources[2][:, None] - targets[2][None, :]
    distance = delta_x * delta_x + delta_y * delta_y + delta_z * delta_z + sources[6][:, None] + targets[6][None, :]
    alignment = sources[3][:, None] * targets[3][None, :] + sources[4][:, None] * targets[4][None, :] + sources[5][:, None] * targets[5][None, :]
    kernel = mu_scale * alignment * lax.rsqrt(distance)
    return jnp.dot(columns.astype(jnp.float32), kernel.astype(jnp.float32), precision=lax.Precision.HIGHEST, preferred_element_type=jnp.float32)

def reference(filament_slot, wire_radius, strand_radius, test_matrix):
    strand = (filament_slot // SEGMENTS).astype(jnp.int32)
    segment = (filament_slot % SEGMENTS).astype(jnp.int32)
    strand_count = strand_radius.shape[0]
    radius = strand_radius[strand]
    height = (segment.astype(jnp.float32) + 0.5) / SEGMENTS
    phase = 2.0 * math.pi / strand_count * strand.astype(jnp.float32)
    twist_angle = phase + twist_rate * height
    cosine_part = jnp.cos(twist_angle)
    sine_part = jnp.sin(twist_angle)
    geometry = jnp.stack([radius * cosine_part, radius * sine_part, height, -twist_rate * radius * sine_part, twist_rate * radius * cosine_part, jnp.ones_like(height), wire_radius * wire_radius])
    source_count = geometry.shape[1]
    block_len = math.gcd(source_count, 2048)
    block_count = source_count // block_len
    geo_blocks = geometry.reshape(7, block_count, block_len).transpose(1, 0, 2)
    col_blocks = test_matrix.reshape(RANK, block_count, block_len).transpose(1, 0, 2)

    def per_target(target_block):

        def step_once(running, pieces):
            return (running + source_block(target_block, pieces[0], pieces[1]), None)
        running, _ = lax.scan(step_once, jnp.zeros((RANK, block_len), jnp.float32), (geo_blocks, col_blocks))
        return running
    sketch = lax.map(per_target, geo_blocks)
    sketch = sketch.transpose(1, 0, 2).reshape(RANK, source_count)
    gram_matrix = jnp.dot(sketch.astype(jnp.float32), sketch.T.astype(jnp.float32), precision=lax.Precision.HIGHEST, preferred_element_type=jnp.float32)
    cholesky_low = jnp.linalg.cholesky(gram_matrix)
    solved = jax.scipy.linalg.solve_triangular(cholesky_low, sketch, lower=True)
    scale_root = math.sqrt(source_count)
    return (solved * scale_root, cholesky_low.T / scale_root)
```

```python
import functools
import math

import jax
import jax.numpy as jnp
from jax import lax
from jax.experimental import pallas as pl
from jax.experimental.pallas import tpu as pltpu
from jax.sharding import PartitionSpec as P

SEGMENTS = 128
GEO_ROWS = 8
MU_SCALE = 1e-05
TWIST_RATE = 4.0 * math.pi
FOLDED = MU_SCALE * TWIST_RATE * TWIST_RATE / 2.0
OFFSET = 2.0 / (TWIST_RATE * TWIST_RATE)
MESH = pl.DeviceIdType.MESH


def local_geometry(slot, wire, strand_radius):
    strand = slot // SEGMENTS
    segment = slot % SEGMENTS
    strand_count = strand_radius.shape[1]
    count = slot.shape[1]
    onehot = (
        lax.broadcasted_iota(jnp.int32, (strand_count, count), 0) == strand
    ).astype(jnp.float32)
    radius = jnp.dot(
        jnp.broadcast_to(strand_radius, (8, strand_count)),
        onehot,
        precision=lax.Precision.HIGHEST,
        preferred_element_type=jnp.float32,
    )[0:1]
    height = (segment.astype(jnp.float32) + 0.5) / SEGMENTS
    angle = 2.0 * math.pi / strand_count * strand.astype(jnp.float32) + TWIST_RATE * height
    root = math.sqrt(2.0)
    x = root * radius * jnp.cos(angle)
    y = root * radius * jnp.sin(angle)
    z = root * (height - 0.5)
    e = 0.5 * (x * x + y * y + z * z) + wire * wire
    return jnp.concatenate([x, y, z, e, x, y, z, e], axis=0)


def sketch_kernel(
    dims, slot_ref, wire_ref, radius_ref, test_ref, sketch_ref, gram_ref,
    pay, tgeo, columns, halves, partial, landed, gram_plane, gram_line,
    pay_send, pay_recv, geo_send, geo_recv, sum_send, sum_recv,
    gp_send, gp_recv, gl_send, gl_recv,
):
    rows, cols, subs = dims
    plane = cols * subs
    rank, count = test_ref.shape
    row, col, sub = lax.axis_index("row"), lax.axis_index("col"), lax.axis_index("sub")

    def plane_peer(o):
        return {
            "col": lax.rem(col + o // subs, cols),
            "sub": lax.rem(sub + o % subs, subs),
        }

    def opposite(o):
        return (cols - o // subs) % cols * subs + (subs - o % subs) % subs

    def line_peer(k):
        return {"row": lax.rem(row + k, rows)}

    barrier = pltpu.get_barrier_semaphore()
    for o in range(1, plane):
        pl.semaphore_signal(barrier, inc=1, device_id=plane_peer(o), device_id_type=MESH)
    for k in range(1, rows):
        pl.semaphore_signal(barrier, inc=1, device_id=line_peer(k), device_id_type=MESH)

    geo = local_geometry(slot_ref[...], wire_ref[...], radius_ref[...])
    pay[0, :rank, :] = test_ref[...]
    pay[0, rank:, :] = geo
    tgeo[0] = geo
    pl.semaphore_wait(barrier, plane + rows - 2)

    def copy_geo(o):
        return pltpu.make_async_remote_copy(
            src_ref=pay.at[0, pl.ds(rank, GEO_ROWS)], dst_ref=tgeo.at[opposite(o)],
            send_sem=geo_send.at[o], recv_sem=geo_recv.at[opposite(o)],
            device_id=plane_peer(o), device_id_type=MESH,
        )

    def copy_pay(k):
        return pltpu.make_async_remote_copy(
            src_ref=pay.at[0], dst_ref=pay.at[k],
            send_sem=pay_send.at[k], recv_sem=pay_recv.at[k],
            device_id=line_peer(k), device_id_type=MESH,
        )

    def copy_sum(o):
        return pltpu.make_async_remote_copy(
            src_ref=partial.at[o], dst_ref=landed.at[o],
            send_sem=sum_send.at[o], recv_sem=sum_recv.at[o],
            device_id=plane_peer(o), device_id_type=MESH,
        )

    def order(index):
        return (index + 1) // 2 if index % 2 else (rows - index // 2) % rows

    for o in reversed(range(1, plane)):
        copy_geo(o).start()
    for index in range(1, rows):
        copy_pay(order(index)).start()

    def prepare(k):
        columns[...] = jnp.concatenate(
            [pay[k, rank:, :]] * (128 // GEO_ROWS), axis=0
        ).T
        test = pay[k, :rank, :]
        high = test.astype(jnp.bfloat16)
        halves[:rank, :] = high
        halves[rank:, :] = (test - high.astype(jnp.float32)).astype(jnp.bfloat16)

    def block(o, first):
        xs, ys = columns[:, 0:1], columns[:, 1:2]
        zs, es = columns[:, 2:3], columns[:, 3:4]
        xt, yt = tgeo[o, 0:1, :], tgeo[o, 1:2, :]
        zt, et = tgeo[o, 2:3, :], tgeo[o, 3:4, :]
        cross = xs * xt + ys * yt
        distance = (es + et) - cross - zs * zt
        kernel = (cross + OFFSET) * lax.rsqrt(distance)
        high = kernel.astype(jnp.bfloat16)
        low = (kernel - high.astype(jnp.float32)).astype(jnp.bfloat16)
        both = jnp.dot(halves[...], high, preferred_element_type=jnp.float32)
        rest = jnp.dot(halves[:rank, :], low, preferred_element_type=jnp.float32)
        term = both[:rank] + (both[rank:] + rest)
        if first:
            partial[o] = term
        else:
            partial[o] += term

    prepare(0)
    block(0, True)
    for o in range(1, plane):
        copy_geo(opposite(o)).wait_recv()

    @pl.loop(1, plane)
    def _(o):
        block(o, True)

    for index in range(1, rows - 1):
        copy_pay(order(index)).wait_recv()
        prepare(order(index))

        @pl.loop(0, plane)
        def _(o):
            block(o, False)

    copy_pay(order(rows - 1)).wait_recv()
    prepare(order(rows - 1))
    for o in reversed(range(1, plane)):
        block(o, False)
        copy_sum(o).start()
    block(0, False)
    sketch = partial[0]
    for o in range(1, plane):
        copy_sum(o).wait_recv()
        sketch = sketch + landed[o]
    sketch_ref[...] = sketch

    gram = lax.dot_general(
        sketch, sketch, (((1,), (1,)), ((), ())),
        precision=lax.Precision.HIGHEST, preferred_element_type=jnp.float32,
    )
    place = col * subs + sub
    gram_plane[place] = gram

    def copy_gp(o):
        return pltpu.make_async_remote_copy(
            src_ref=gram_plane.at[place], dst_ref=gram_plane.at[place],
            send_sem=gp_send.at[o], recv_sem=gp_recv.at[o],
            device_id=plane_peer(o), device_id_type=MESH,
        )

    def copy_gl(k):
        return pltpu.make_async_remote_copy(
            src_ref=gram_line.at[row], dst_ref=gram_line.at[row],
            send_sem=gl_send.at[k], recv_sem=gl_recv.at[k],
            device_id=line_peer(k), device_id_type=MESH,
        )

    for o in range(1, plane):
        copy_gp(o).start()
    for o in range(1, plane):
        copy_gp(o).wait()
    total = gram_plane[0]
    for o in range(1, plane):
        total = total + gram_plane[o]
    gram_line[row] = total
    for k in range(1, rows):
        copy_gl(k).start()
    for k in range(1, rows):
        copy_gl(k).wait()
    total = gram_line[0]
    for k in range(1, rows):
        total = total + gram_line[k]
    gram_ref[...] = total

    for o in range(1, plane):
        copy_geo(o).wait_send()
        copy_sum(o).wait_send()
    for k in range(1, rows):
        copy_pay(k).wait_send()


def factor_kernel(scale, sketch_ref, gram_ref, basis_ref, factor_ref):
    rank = gram_ref.shape[0]
    tiles = rank // 8
    eye = (
        lax.broadcasted_iota(jnp.int32, (rank, rank), 0)
        == lax.broadcasted_iota(jnp.int32, (rank, rank), 1)
    ).astype(jnp.float32)
    wide = jnp.concatenate([gram_ref[...], eye], axis=1)
    parts = [wide[8 * t : 8 * t + 8] for t in range(tiles)]
    place = lax.broadcasted_iota(jnp.int32, (8, 2 * rank), 0)
    for j in range(rank):
        own, line = divmod(j, 8)
        pivot_row = parts[own][line : line + 1]
        scaled = pivot_row * (1.0 / pivot_row[:, j : j + 1])
        for t in range(own, tiles):
            update = parts[t][:, j : j + 1] * scaled
            if t == own:
                update = jnp.where(place > line, update, 0.0)
            parts[t] = parts[t] - update
    wide = jnp.concatenate(parts, axis=0)
    pivots = jnp.sum(wide[:, :rank] * eye, axis=1, keepdims=True)
    wide = wide * lax.rsqrt(pivots)
    upper = (
        lax.broadcasted_iota(jnp.int32, (rank, rank), 0)
        <= lax.broadcasted_iota(jnp.int32, (rank, rank), 1)
    )
    factor_ref[...] = jnp.where(upper, wide[:, :rank], 0.0) * (FOLDED / scale)
    basis_ref[...] = jnp.dot(
        wide[:, rank:] * scale, sketch_ref[...],
        precision=lax.Precision.HIGHEST, preferred_element_type=jnp.float32,
    )


def per_device(filament_slot, wire_radius, strand_radius, test_matrix):
    dims = tuple(lax.axis_size(name) for name in ("row", "col", "sub"))
    rows, plane = dims[0], dims[1] * dims[2]
    rank, count = test_matrix.shape
    vmem = pl.BlockSpec(memory_space=pltpu.VMEM)
    f32 = jnp.float32
    dma = pltpu.SemaphoreType.DMA
    sketch, gram = pl.pallas_call(
        functools.partial(sketch_kernel, dims),
        out_shape=(
            jax.ShapeDtypeStruct((rank, count), f32),
            jax.ShapeDtypeStruct((rank, rank), f32),
        ),
        in_specs=[vmem] * 4,
        out_specs=(vmem, vmem),
        scratch_shapes=[
            pltpu.VMEM((rows, rank + GEO_ROWS, count), f32),
            pltpu.VMEM((plane, GEO_ROWS, count), f32),
            pltpu.VMEM((count, 128), f32),
            pltpu.VMEM((2 * rank, count), jnp.bfloat16),
            pltpu.VMEM((plane, rank, count), f32),
            pltpu.VMEM((plane, rank, count), f32),
            pltpu.VMEM((plane, rank, rank), f32),
            pltpu.VMEM((rows, rank, rank), f32),
            dma((rows,)), dma((rows,)), dma((plane,)), dma((plane,)), dma((plane,)), dma((plane,)),
            dma((plane,)), dma((plane,)), dma((rows,)), dma((rows,)),
        ],
        compiler_params=pltpu.CompilerParams(
            collective_id=0, has_side_effects=True, vmem_limit_bytes=48 * 1024 * 1024
        ),
    )(
        filament_slot.reshape(1, count),
        wire_radius.reshape(1, count),
        strand_radius.reshape(1, -1),
        test_matrix,
    )
    scale = math.sqrt(count * rows * plane)
    return pl.pallas_call(
        functools.partial(factor_kernel, scale),
        out_shape=(
            jax.ShapeDtypeStruct((rank, count), f32),
            jax.ShapeDtypeStruct((rank, rank), f32),
        ),
        in_specs=[vmem] * 2,
        out_specs=(vmem, vmem),
        compiler_params=pltpu.CompilerParams(vmem_limit_bytes=16 * 1024 * 1024),
    )(sketch, gram)


def solution(mesh):
    return jax.shard_map(
        per_device,
        mesh=mesh,
        in_specs=(
            P(("grp", "row", "col", "sub")),
            P(("grp", "row", "col", "sub")),
            P("grp"),
            P(None, ("grp", "row", "col", "sub")),
        ),
        out_specs=(P(None, ("grp", "row", "col", "sub")), P("grp", None)),
        check_vma=False,
    )
```

```python
import functools
import math

import jax
import jax.numpy as jnp
from jax import lax
from jax.experimental import pallas as pl
from jax.experimental.pallas import tpu as pltpu
from jax.sharding import PartitionSpec as P

SEGMENTS = 128
GEO_ROWS = 8
MU_SCALE = 1e-05
TWIST_RATE = 4.0 * math.pi
FOLDED = MU_SCALE * TWIST_RATE * TWIST_RATE / 2.0
OFFSET = 2.0 / (TWIST_RATE * TWIST_RATE)
MESH = pl.DeviceIdType.MESH


def local_geometry(slot, wire, strand_radius):
    strand = slot // SEGMENTS
    segment = slot % SEGMENTS
    strand_count = strand_radius.shape[1]
    count = slot.shape[1]
    onehot = (
        lax.broadcasted_iota(jnp.int32, (strand_count, count), 0) == strand
    ).astype(jnp.float32)
    radius = jnp.dot(
        jnp.broadcast_to(strand_radius, (8, strand_count)),
        onehot,
        precision=lax.Precision.HIGHEST,
        preferred_element_type=jnp.float32,
    )[0:1]
    height = (segment.astype(jnp.float32) + 0.5) / SEGMENTS
    angle = 2.0 * math.pi / strand_count * strand.astype(jnp.float32) + TWIST_RATE * height
    root = math.sqrt(2.0)
    x = root * radius * jnp.cos(angle)
    y = root * radius * jnp.sin(angle)
    z = root * (height - 0.5)
    e = 0.5 * (x * x + y * y + z * z) + wire * wire
    return jnp.concatenate([x, y, z, e, x, y, z, e], axis=0)


def sketch_kernel(
    dims, slot_hbm, wire_hbm, radius_hbm, test_hbm, sketch_ref, gram_ref,
    slot_ref, wire_ref, radius_ref,
    pay, tgeo, columns, halves, partial, landed, gram_plane, gram_line, load_sem,
    pay_send, pay_recv, fwd_send, fwd_recv, geo_send, geo_recv, sum_send, sum_recv,
    gp_send, gp_recv, gl_send, gl_recv,
):
    rows, cols, subs = dims
    plane = cols * subs
    rank, count = test_hbm.shape
    row, col, sub = lax.axis_index("row"), lax.axis_index("col"), lax.axis_index("sub")

    def plane_peer(o):
        return {
            "col": lax.rem(col + o // subs, cols),
            "sub": lax.rem(sub + o % subs, subs),
        }

    def line_peer(k):
        return {"row": lax.rem(row + k, rows)}

    def col_peer(o):
        return {"col": lax.rem(col + o, cols)}

    loads = [
        pltpu.make_async_copy(slot_hbm, slot_ref, load_sem.at[0]),
        pltpu.make_async_copy(wire_hbm, wire_ref, load_sem.at[1]),
        pltpu.make_async_copy(radius_hbm, radius_ref, load_sem.at[2]),
        pltpu.make_async_copy(test_hbm, pay.at[0, 0, pl.ds(0, rank)], load_sem.at[3]),
    ]
    for load in loads:
        load.start()
    barrier = pltpu.get_barrier_semaphore()
    for o in range(1, plane):
        pl.semaphore_signal(barrier, inc=1, device_id=plane_peer(o), device_id_type=MESH)
    for k in range(1, rows):
        pl.semaphore_signal(barrier, inc=1, device_id=line_peer(k), device_id_type=MESH)

    for load in loads[:3]:
        load.wait()
    geo = local_geometry(slot_ref[...], wire_ref[...], radius_ref[...])
    pay[0, 0, rank:, :] = geo
    tgeo[0] = geo
    partial[...] = jnp.zeros_like(partial)
    loads[3].wait()
    pl.semaphore_wait(barrier, plane + rows - 2)

    def copy_geo(o):
        return pltpu.make_async_remote_copy(
            src_ref=pay.at[0, 0, pl.ds(rank, GEO_ROWS)], dst_ref=tgeo.at[cols - o],
            send_sem=geo_send.at[o], recv_sem=geo_recv.at[cols - o],
            device_id=col_peer(o), device_id_type=MESH,
        )

    def copy_pay(k):
        return pltpu.make_async_remote_copy(
            src_ref=pay.at[0, 0], dst_ref=pay.at[0, k],
            send_sem=pay_send.at[k], recv_sem=pay_recv.at[k],
            device_id=line_peer(k), device_id_type=MESH,
        )

    def copy_fwd(s, k):
        return pltpu.make_async_remote_copy(
            src_ref=pay.at[0, k], dst_ref=pay.at[subs - s, k],
            send_sem=fwd_send.at[s, k], recv_sem=fwd_recv.at[subs - s, k],
            device_id={"sub": lax.rem(sub + s, subs)}, device_id_type=MESH,
        )

    def copy_sum(o):
        return pltpu.make_async_remote_copy(
            src_ref=partial.at[o], dst_ref=landed.at[o],
            send_sem=sum_send.at[o], recv_sem=sum_recv.at[o],
            device_id=col_peer(o), device_id_type=MESH,
        )

    def order(index):
        odd = index % 2
        return odd * ((index + 1) // 2) + (1 - odd) * ((rows - index // 2) % rows)

    for o in range(1, cols):
        copy_geo(o).start()
    for index in range(1, rows):
        copy_pay(order(index)).start()
    for s in range(1, subs):
        copy_fwd(s, 0).start()

    def prepare(s, k):
        columns[s, k] = jnp.concatenate(
            [pay[s, k, rank:, :]] * (128 // GEO_ROWS), axis=0
        ).T
        test = pay[s, k, :rank, :]
        high = test.astype(jnp.bfloat16)
        halves[s, k, :rank, :] = high
        halves[s, k, rank:, :] = (test - high.astype(jnp.float32)).astype(jnp.bfloat16)

    def block(s, k, o):
        xs, ys = columns[s, k, :, 0:1], columns[s, k, :, 1:2]
        zs, es = columns[s, k, :, 2:3], columns[s, k, :, 3:4]
        xt, yt = tgeo[o, 0:1, :], tgeo[o, 1:2, :]
        zt, et = tgeo[o, 2:3, :], tgeo[o, 3:4, :]
        cross = xs * xt + ys * yt
        distance = (es + et) - cross - zs * zt
        kernel = (cross + OFFSET) * lax.rsqrt(distance)
        high = kernel.astype(jnp.bfloat16)
        low = (kernel - high.astype(jnp.float32)).astype(jnp.bfloat16)
        both = jnp.dot(halves[s, k], high, preferred_element_type=jnp.float32)
        rest = jnp.dot(halves[s, k, :rank, :], low, preferred_element_type=jnp.float32)
        partial[o] += both[:rank] + (both[rank:] + rest)

    late = max(rows - 2, 0)

    @pl.loop(0, rows)
    def _(index):
        k = order(index)

        @pl.when(index > 0)
        def _():
            copy_pay(k).wait_recv()
            for s in range(1, subs):
                copy_fwd(s, k).start()

        @pl.when(index == 0)
        def _():
            for o in range(1, cols):
                copy_geo(cols - o).wait_recv()

        @pl.loop(0, subs)
        def _(s):
            @pl.when(s > 0)
            def _():
                copy_fwd(subs - s, k).wait_recv()

            prepare(s, k)

            @pl.loop(1, cols)
            def _(o):
                block(s, k, o)

            @pl.when(index < late)
            def _():
                block(s, k, 0)

    for o in range(1, cols):
        copy_sum(o).start()

    @pl.loop(late, rows)
    def _(index):
        @pl.loop(0, subs)
        def _(s):
            block(s, order(index), 0)

    sketch = partial[0]
    for o in range(1, cols):
        copy_sum(o).wait_recv()
        sketch = sketch + landed[o]
    sketch_ref[...] = sketch

    gram = lax.dot_general(
        sketch, sketch, (((1,), (1,)), ((), ())),
        precision=lax.Precision.HIGHEST, preferred_element_type=jnp.float32,
    )
    place = col * subs + sub
    gram_plane[place] = jnp.concatenate([gram[: rank // 2], gram[rank // 2 :]], axis=1)

    def copy_gp(o):
        return pltpu.make_async_remote_copy(
            src_ref=gram_plane.at[place], dst_ref=gram_plane.at[place],
            send_sem=gp_send.at[o], recv_sem=gp_recv.at[o],
            device_id=plane_peer(o), device_id_type=MESH,
        )

    def copy_gl(k):
        return pltpu.make_async_remote_copy(
            src_ref=gram_line.at[row], dst_ref=gram_line.at[row],
            send_sem=gl_send.at[k], recv_sem=gl_recv.at[k],
            device_id=line_peer(k), device_id_type=MESH,
        )

    for o in reversed(range(1, plane)):
        copy_gp(o).start()
    for o in range(1, plane):
        copy_gp(o).wait_recv()
    total = gram_plane[0]
    for o in range(1, plane):
        total = total + gram_plane[o]
    gram_line[row] = total
    for k in range(1, rows):
        copy_gl(k).start()
    for o in range(1, plane):
        copy_gp(o).wait_send()
    for o in range(1, cols):
        copy_geo(o).wait_send()
        copy_sum(o).wait_send()
    for k in range(1, rows):
        copy_pay(k).wait_send()
    for s in range(1, subs):
        for k in range(rows):
            copy_fwd(s, k).wait_send()
    for k in range(1, rows):
        copy_gl(k).wait_recv()
    total = gram_line[0]
    for k in range(1, rows):
        total = total + gram_line[k]
    gram_ref[...] = total
    for k in range(1, rows):
        copy_gl(k).wait_send()


def factor_kernel(scale, sketch_ref, gram_ref, basis_ref, factor_ref):
    rank = gram_ref.shape[1] // 2
    tiles = rank // 8
    eye = (
        lax.broadcasted_iota(jnp.int32, (rank, rank), 0)
        == lax.broadcasted_iota(jnp.int32, (rank, rank), 1)
    ).astype(jnp.float32)
    gram = jnp.concatenate([gram_ref[:, :rank], gram_ref[:, rank:]], axis=0)
    wide = jnp.concatenate([gram, eye], axis=1)
    parts = [wide[8 * t : 8 * t + 8] for t in range(tiles)]
    for own in range(tiles):
        base = 8 * own
        lines = [jnp.broadcast_to(parts[own][a : a + 1], (8, 2 * rank)) for a in range(8)]
        inner = {
            (a, b): jnp.broadcast_to(lines[a][:, base + b : base + b + 1], (8, 2 * rank))
            for a in range(8)
            for b in range(a, 8)
        }
        ratio = {}
        for a in range(8):
            inverse = 1.0 / inner[a, a]
            for b in range(a + 1, 8):
                ratio[a, b] = inner[a, b] * inverse
                for c in range(b, 8):
                    inner[b, c] = inner[b, c] - ratio[a, b] * inner[a, c]
                lines[b] = lines[b] - ratio[a, b] * lines[a]
            ratio[a, a] = inverse
        scaled = [lines[a] * ratio[a, a] for a in range(8)]
        for t in range(own + 1, tiles):
            heads = [
                jnp.broadcast_to(parts[t][:, base + a : base + a + 1], (8, 2 * rank))
                for a in range(8)
            ]
            for a in range(8):
                for b in range(a + 1, 8):
                    heads[b] = heads[b] - ratio[a, b] * heads[a]
            terms = [heads[a] * scaled[a] for a in range(8)]
            while len(terms) > 1:
                terms = [terms[i] + terms[i + 1] for i in range(0, len(terms), 2)]
            parts[t] = parts[t] - terms[0]
        parts[own] = jnp.concatenate([lines[a][a : a + 1] for a in range(8)], axis=0)
    wide = jnp.concatenate(parts, axis=0)
    pivots = jnp.sum(wide[:, :rank] * eye, axis=1, keepdims=True)
    wide = wide * lax.rsqrt(pivots)
    upper = (
        lax.broadcasted_iota(jnp.int32, (rank, rank), 0)
        <= lax.broadcasted_iota(jnp.int32, (rank, rank), 1)
    )
    factor_ref[...] = jnp.where(upper, wide[:, :rank], 0.0) * (FOLDED / scale)
    basis_ref[...] = jnp.dot(
        wide[:, rank:] * scale, sketch_ref[...],
        precision=lax.Precision.HIGHEST, preferred_element_type=jnp.float32,
    )


def per_device(filament_slot, wire_radius, strand_radius, test_matrix):
    dims = tuple(lax.axis_size(name) for name in ("row", "col", "sub"))
    rows, cols, subs = dims
    plane = cols * subs
    rank, count = test_matrix.shape
    vmem = pl.BlockSpec(memory_space=pltpu.VMEM)
    hbm = pl.BlockSpec(memory_space=pltpu.HBM)
    f32 = jnp.float32
    dma = pltpu.SemaphoreType.DMA
    sketch, gram = pl.pallas_call(
        functools.partial(sketch_kernel, dims),
        out_shape=(
            jax.ShapeDtypeStruct((rank, count), f32),
            jax.ShapeDtypeStruct((rank // 2, 2 * rank), f32),
        ),
        in_specs=[hbm] * 4,
        out_specs=(vmem, vmem),
        scratch_shapes=[
            pltpu.VMEM((1, count), jnp.int32),
            pltpu.VMEM((1, count), f32),
            pltpu.VMEM((1, strand_radius.shape[0]), f32),
            pltpu.VMEM((subs, rows, rank + GEO_ROWS, count), f32),
            pltpu.VMEM((cols, GEO_ROWS, count), f32),
            pltpu.VMEM((subs, rows, count, 128), f32),
            pltpu.VMEM((subs, rows, 2 * rank, count), jnp.bfloat16),
            pltpu.VMEM((cols, rank, count), f32),
            pltpu.VMEM((cols, rank, count), f32),
            pltpu.VMEM((plane, rank // 2, 2 * rank), f32),
            pltpu.VMEM((rows, rank // 2, 2 * rank), f32),
            dma((4,)),
            dma((rows,)), dma((rows,)), dma((subs, rows)), dma((subs, rows)),
            dma((cols,)), dma((cols,)), dma((cols,)), dma((cols,)),
            dma((plane,)), dma((plane,)), dma((rows,)), dma((rows,)),
        ],
        compiler_params=pltpu.CompilerParams(
            collective_id=0, has_side_effects=True, vmem_limit_bytes=48 * 1024 * 1024
        ),
    )(
        filament_slot.reshape(1, count),
        wire_radius.reshape(1, count),
        strand_radius.reshape(1, -1),
        test_matrix,
    )
    scale = math.sqrt(count * rows * plane)
    return pl.pallas_call(
        functools.partial(factor_kernel, scale),
        out_shape=(
            jax.ShapeDtypeStruct((rank, count), f32),
            jax.ShapeDtypeStruct((rank, rank), f32),
        ),
        in_specs=[vmem] * 2,
        out_specs=(vmem, vmem),
        compiler_params=pltpu.CompilerParams(vmem_limit_bytes=16 * 1024 * 1024),
    )(sketch, gram)


def solution(mesh):
    return jax.shard_map(
        per_device,
        mesh=mesh,
        in_specs=(
            P(("grp", "row", "col", "sub")),
            P(("grp", "row", "col", "sub")),
            P("grp"),
            P(None, ("grp", "row", "col", "sub")),
        ),
        out_specs=(P(None, ("grp", "row", "col", "sub")), P("grp", None)),
        check_vma=False,
    )
```

```python
import functools
import math

import jax
import jax.numpy as jnp
from jax import lax
from jax.experimental import pallas as pl
from jax.experimental.pallas import tpu as pltpu
from jax.sharding import PartitionSpec as P

SEGMENTS = 128
GEO_ROWS = 8
MU_SCALE = 1e-05
TWIST_RATE = 4.0 * math.pi
FOLDED = MU_SCALE * TWIST_RATE * TWIST_RATE / 2.0
OFFSET = 2.0 / (TWIST_RATE * TWIST_RATE)
MESH = pl.DeviceIdType.MESH


def local_geometry(slot, wire, strand_radius):
    strand = slot // SEGMENTS
    segment = slot % SEGMENTS
    strand_count = strand_radius.shape[1]
    count = slot.shape[1]
    onehot = (
        lax.broadcasted_iota(jnp.int32, (strand_count, count), 0) == strand
    ).astype(jnp.float32)
    radius = jnp.dot(
        jnp.broadcast_to(strand_radius, (8, strand_count)),
        onehot,
        precision=lax.Precision.HIGHEST,
        preferred_element_type=jnp.float32,
    )[0:1]
    height = (segment.astype(jnp.float32) + 0.5) / SEGMENTS
    angle = 2.0 * math.pi / strand_count * strand.astype(jnp.float32) + TWIST_RATE * height
    root = math.sqrt(2.0)
    x = root * radius * jnp.cos(angle)
    y = root * radius * jnp.sin(angle)
    z = root * (height - 0.5)
    e = 0.5 * (x * x + y * y + z * z) + wire * wire
    return jnp.concatenate([x, y, z, e, x, y, z, e], axis=0)


def split_rows(rows):
    count = 2 if rows % 2 == 0 else 1
    return rows // count, count


def sketch_kernel(
    dims, slot_hbm, wire_hbm, radius_hbm, test_hbm, sketch_ref, gram_ref,
    slot_ref, wire_ref, radius_ref,
    pay, tgeo, columns, halves, partial, landed, gram_plane, gram_line, load_sem,
    pay_send, pay_recv, fwd_send, fwd_recv, geo_send, geo_recv, sum_send, sum_recv,
    gp_send, gp_recv, gl_send, gl_recv,
):
    rows, cols, subs = dims
    plane = cols * subs
    near, halves_count = split_rows(rows)
    line = near * cols
    rank, count = test_hbm.shape
    row, col, sub = lax.axis_index("row"), lax.axis_index("col"), lax.axis_index("sub")

    def plane_peer(o):
        return {
            "col": lax.rem(col + o // subs, cols),
            "sub": lax.rem(sub + o % subs, subs),
        }

    def row_peer(k):
        return {"row": lax.rem(row + k, rows)}

    def line_peer(k):
        return {
            "row": row // near * near + lax.rem(row + k // cols, near),
            "col": lax.rem(col + k % cols, cols),
        }

    def half_peer(o):
        return {"row": lax.rem(row + o * near, rows)}

    loads = [
        pltpu.make_async_copy(slot_hbm, slot_ref, load_sem.at[0]),
        pltpu.make_async_copy(wire_hbm, wire_ref, load_sem.at[1]),
        pltpu.make_async_copy(radius_hbm, radius_ref, load_sem.at[2]),
        pltpu.make_async_copy(test_hbm, pay.at[0, 0, pl.ds(0, rank)], load_sem.at[3]),
    ]
    for load in loads:
        load.start()
    barrier = pltpu.get_barrier_semaphore()
    for o in range(1, plane):
        pl.semaphore_signal(barrier, inc=1, device_id=plane_peer(o), device_id_type=MESH)
    for k in range(1, rows):
        pl.semaphore_signal(barrier, inc=1, device_id=row_peer(k), device_id_type=MESH)
    across = [k for k in range(1, line) if k // cols and k % cols]
    for k in across:
        pl.semaphore_signal(barrier, inc=1, device_id=line_peer(k), device_id_type=MESH)

    for load in loads[:3]:
        load.wait()
    geo = local_geometry(slot_ref[...], wire_ref[...], radius_ref[...])
    pay[0, 0, rank:, :] = geo
    tgeo[0] = geo
    partial[...] = jnp.zeros_like(partial)
    loads[3].wait()
    pl.semaphore_wait(barrier, plane + rows - 2 + len(across))

    def copy_geo(o):
        return pltpu.make_async_remote_copy(
            src_ref=pay.at[0, 0, pl.ds(rank, GEO_ROWS)], dst_ref=tgeo.at[halves_count - o],
            send_sem=geo_send.at[o], recv_sem=geo_recv.at[halves_count - o],
            device_id=half_peer(o), device_id_type=MESH,
        )

    def copy_pay(k):
        return pltpu.make_async_remote_copy(
            src_ref=pay.at[0, 0], dst_ref=pay.at[0, k],
            send_sem=pay_send.at[k], recv_sem=pay_recv.at[k],
            device_id=line_peer(k), device_id_type=MESH,
        )

    def copy_fwd(s, k):
        return pltpu.make_async_remote_copy(
            src_ref=pay.at[0, k], dst_ref=pay.at[subs - s, k],
            send_sem=fwd_send.at[s, k], recv_sem=fwd_recv.at[subs - s, k],
            device_id={"sub": lax.rem(sub + s, subs)}, device_id_type=MESH,
        )

    def copy_sum(o):
        return pltpu.make_async_remote_copy(
            src_ref=partial.at[o], dst_ref=landed.at[o],
            send_sem=sum_send.at[o], recv_sem=sum_recv.at[o],
            device_id=half_peer(o), device_id_type=MESH,
        )

    for o in range(1, halves_count):
        copy_geo(o).start()
    for k in range(1, line):
        copy_pay(k).start()
    for s in range(1, subs):
        copy_fwd(s, 0).start()

    def prepare(s, k):
        columns[s, k] = jnp.concatenate(
            [pay[s, k, rank:, :]] * (128 // GEO_ROWS), axis=0
        ).T
        test = pay[s, k, :rank, :]
        high = test.astype(jnp.bfloat16)
        halves[s, k, :rank, :] = high
        halves[s, k, rank:, :] = (test - high.astype(jnp.float32)).astype(jnp.bfloat16)

    def block(s, k, o):
        xs, ys = columns[s, k, :, 0:1], columns[s, k, :, 1:2]
        zs, es = columns[s, k, :, 2:3], columns[s, k, :, 3:4]
        xt, yt = tgeo[o, 0:1, :], tgeo[o, 1:2, :]
        zt, et = tgeo[o, 2:3, :], tgeo[o, 3:4, :]
        cross = xs * xt + ys * yt
        distance = (es + et) - cross - zs * zt
        kernel = (cross + OFFSET) * lax.rsqrt(distance)
        high = kernel.astype(jnp.bfloat16)
        low = (kernel - high.astype(jnp.float32)).astype(jnp.bfloat16)
        both = jnp.dot(halves[s, k], high, preferred_element_type=jnp.float32)
        rest = jnp.dot(halves[s, k, :rank, :], low, preferred_element_type=jnp.float32)
        partial[o] += both[:rank] + (both[rank:] + rest)

    late = 1

    @pl.loop(0, line)
    def _(k):
        @pl.when(k > 0)
        def _():
            copy_pay(k).wait_recv()
            for s in range(1, subs):
                copy_fwd(s, k).start()

        @pl.when(k == 0)
        def _():
            for o in range(1, halves_count):
                copy_geo(halves_count - o).wait_recv()

        @pl.loop(0, subs)
        def _(s):
            @pl.when(s > 0)
            def _():
                copy_fwd(subs - s, k).wait_recv()

            prepare(s, k)

            @pl.loop(1, halves_count)
            def _(o):
                block(s, k, o)

            @pl.when(k < late)
            def _():
                block(s, k, 0)

    for o in range(1, halves_count):
        copy_sum(o).start()

    @pl.loop(late, line)
    def _(k):
        @pl.loop(0, subs)
        def _(s):
            block(s, k, 0)

    sketch = partial[0]
    for o in range(1, halves_count):
        copy_sum(o).wait_recv()
        sketch = sketch + landed[o]
    sketch_ref[...] = sketch

    gram = lax.dot_general(
        sketch, sketch, (((1,), (1,)), ((), ())),
        precision=lax.Precision.HIGHEST, preferred_element_type=jnp.float32,
    )
    place = col * subs + sub
    gram_plane[place] = jnp.concatenate([gram[: rank // 2], gram[rank // 2 :]], axis=1)

    def copy_gp(o):
        return pltpu.make_async_remote_copy(
            src_ref=gram_plane.at[place], dst_ref=gram_plane.at[place],
            send_sem=gp_send.at[o], recv_sem=gp_recv.at[o],
            device_id=plane_peer(o), device_id_type=MESH,
        )

    def copy_gl(k):
        return pltpu.make_async_remote_copy(
            src_ref=gram_line.at[row], dst_ref=gram_line.at[row],
            send_sem=gl_send.at[k], recv_sem=gl_recv.at[k],
            device_id=row_peer(k), device_id_type=MESH,
        )

    for o in reversed(range(1, plane)):
        copy_gp(o).start()
    for o in range(1, plane):
        copy_gp(o).wait_recv()
    total = gram_plane[0]
    for o in range(1, plane):
        total = total + gram_plane[o]
    gram_line[row] = total
    for k in range(1, rows):
        copy_gl(k).start()
    for o in range(1, plane):
        copy_gp(o).wait_send()
    for o in range(1, halves_count):
        copy_geo(o).wait_send()
        copy_sum(o).wait_send()
    for k in range(1, line):
        copy_pay(k).wait_send()
    for s in range(1, subs):
        for k in range(line):
            copy_fwd(s, k).wait_send()
    for k in range(1, rows):
        copy_gl(k).wait_recv()
    total = gram_line[0]
    for k in range(1, rows):
        total = total + gram_line[k]
    gram_ref[...] = total
    for k in range(1, rows):
        copy_gl(k).wait_send()


def factor_kernel(scale, sketch_ref, gram_ref, basis_ref, factor_ref):
    rank = gram_ref.shape[1] // 2
    tiles = rank // 8
    eye = (
        lax.broadcasted_iota(jnp.int32, (rank, rank), 0)
        == lax.broadcasted_iota(jnp.int32, (rank, rank), 1)
    ).astype(jnp.float32)
    gram = jnp.concatenate([gram_ref[:, :rank], gram_ref[:, rank:]], axis=0)
    wide = jnp.concatenate([gram, eye], axis=1)
    parts = [wide[8 * t : 8 * t + 8] for t in range(tiles)]
    for own in range(tiles):
        base = 8 * own
        lines = [jnp.broadcast_to(parts[own][a : a + 1], (8, 2 * rank)) for a in range(8)]
        inner = {
            (a, b): jnp.broadcast_to(lines[a][:, base + b : base + b + 1], (8, 2 * rank))
            for a in range(8)
            for b in range(a, 8)
        }
        ratio = {}
        for a in range(8):
            inverse = 1.0 / inner[a, a]
            for b in range(a + 1, 8):
                ratio[a, b] = inner[a, b] * inverse
                for c in range(b, 8):
                    inner[b, c] = inner[b, c] - ratio[a, b] * inner[a, c]
                lines[b] = lines[b] - ratio[a, b] * lines[a]
            ratio[a, a] = inverse
        scaled = [lines[a] * ratio[a, a] for a in range(8)]
        for t in range(own + 1, tiles):
            heads = [
                jnp.broadcast_to(parts[t][:, base + a : base + a + 1], (8, 2 * rank))
                for a in range(8)
            ]
            for a in range(8):
                for b in range(a + 1, 8):
                    heads[b] = heads[b] - ratio[a, b] * heads[a]
            terms = [heads[a] * scaled[a] for a in range(8)]
            while len(terms) > 1:
                terms = [terms[i] + terms[i + 1] for i in range(0, len(terms), 2)]
            parts[t] = parts[t] - terms[0]
        parts[own] = jnp.concatenate([lines[a][a : a + 1] for a in range(8)], axis=0)
    wide = jnp.concatenate(parts, axis=0)
    pivots = jnp.sum(wide[:, :rank] * eye, axis=1, keepdims=True)
    wide = wide * lax.rsqrt(pivots)
    upper = (
        lax.broadcasted_iota(jnp.int32, (rank, rank), 0)
        <= lax.broadcasted_iota(jnp.int32, (rank, rank), 1)
    )
    factor_ref[...] = jnp.where(upper, wide[:, :rank], 0.0) * (FOLDED / scale)
    basis_ref[...] = jnp.dot(
        wide[:, rank:] * scale, sketch_ref[...],
        precision=lax.Precision.HIGHEST, preferred_element_type=jnp.float32,
    )


def per_device(filament_slot, wire_radius, strand_radius, test_matrix):
    dims = tuple(lax.axis_size(name) for name in ("row", "col", "sub"))
    rows, cols, subs = dims
    plane = cols * subs
    near, halves_count = split_rows(rows)
    line = near * cols
    rank, count = test_matrix.shape
    vmem = pl.BlockSpec(memory_space=pltpu.VMEM)
    hbm = pl.BlockSpec(memory_space=pltpu.HBM)
    f32 = jnp.float32
    dma = pltpu.SemaphoreType.DMA
    keep = pltpu.with_memory_space_constraint
    sketch, gram = pl.pallas_call(
        functools.partial(sketch_kernel, dims),
        out_shape=(
            jax.ShapeDtypeStruct((rank, count), f32),
            jax.ShapeDtypeStruct((rank // 2, 2 * rank), f32),
        ),
        in_specs=[hbm] * 4,
        out_specs=(vmem, vmem),
        scratch_shapes=[
            pltpu.VMEM((1, count), jnp.int32),
            pltpu.VMEM((1, count), f32),
            pltpu.VMEM((1, strand_radius.shape[0]), f32),
            pltpu.VMEM((subs, line, rank + GEO_ROWS, count), f32),
            pltpu.VMEM((halves_count, GEO_ROWS, count), f32),
            pltpu.VMEM((subs, line, count, 128), f32),
            pltpu.VMEM((subs, line, 2 * rank, count), jnp.bfloat16),
            pltpu.VMEM((halves_count, rank, count), f32),
            pltpu.VMEM((halves_count, rank, count), f32),
            pltpu.VMEM((plane, rank // 2, 2 * rank), f32),
            pltpu.VMEM((rows, rank // 2, 2 * rank), f32),
            dma((4,)),
            dma((line,)), dma((line,)), dma((subs, line)), dma((subs, line)),
            dma((halves_count,)), dma((halves_count,)), dma((halves_count,)), dma((halves_count,)),
            dma((plane,)), dma((plane,)), dma((rows,)), dma((rows,)),
        ],
        compiler_params=pltpu.CompilerParams(
            collective_id=0, has_side_effects=True, vmem_limit_bytes=48 * 1024 * 1024
        ),
    )(
        keep(filament_slot.reshape(1, count), pltpu.HBM),
        keep(wire_radius.reshape(1, count), pltpu.HBM),
        keep(strand_radius.reshape(1, -1), pltpu.HBM),
        keep(test_matrix, pltpu.HBM),
    )
    scale = math.sqrt(count * rows * plane)
    return pl.pallas_call(
        functools.partial(factor_kernel, scale),
        out_shape=(
            jax.ShapeDtypeStruct((rank, count), f32),
            jax.ShapeDtypeStruct((rank, rank), f32),
        ),
        in_specs=[vmem] * 2,
        out_specs=(vmem, vmem),
        compiler_params=pltpu.CompilerParams(vmem_limit_bytes=16 * 1024 * 1024),
    )(sketch, gram)


def solution(mesh):
    return jax.shard_map(
        per_device,
        mesh=mesh,
        in_specs=(
            P(("grp", "row", "col", "sub")),
            P(("grp", "row", "col", "sub")),
            P("grp"),
            P(None, ("grp", "row", "col", "sub")),
        ),
        out_specs=(P(None, ("grp", "row", "col", "sub")), P("grp", None)),
        check_vma=False,
    )
```

```python
import functools
import math

import jax
import jax.numpy as jnp
from jax import lax
from jax.experimental import pallas as pl
from jax.experimental.pallas import tpu as pltpu
from jax.sharding import PartitionSpec as P

SEGMENTS = 128
GEO_ROWS = 8
MU_SCALE = 1e-05
TWIST_RATE = 4.0 * math.pi
FOLDED = MU_SCALE * TWIST_RATE * TWIST_RATE / 2.0
OFFSET = 2.0 / (TWIST_RATE * TWIST_RATE)
MESH = pl.DeviceIdType.MESH


def local_geometry(slot, wire, strand_radius):
    strand = slot // SEGMENTS
    segment = slot % SEGMENTS
    strand_count = strand_radius.shape[1]
    count = slot.shape[1]
    onehot = (
        lax.broadcasted_iota(jnp.int32, (strand_count, count), 0) == strand
    ).astype(jnp.float32)
    radius = jnp.dot(
        jnp.broadcast_to(strand_radius, (8, strand_count)),
        onehot,
        precision=lax.Precision.HIGHEST,
        preferred_element_type=jnp.float32,
    )[0:1]
    height = (segment.astype(jnp.float32) + 0.5) / SEGMENTS
    angle = 2.0 * math.pi / strand_count * strand.astype(jnp.float32) + TWIST_RATE * height
    root = math.sqrt(2.0)
    x = root * radius * jnp.cos(angle)
    y = root * radius * jnp.sin(angle)
    z = root * (height - 0.5)
    e = 0.5 * (x * x + y * y + z * z) + wire * wire
    return jnp.concatenate([x, y, z, e, x, y, z, e], axis=0)


def split_rows(rows):
    count = 2 if rows % 2 == 0 else 1
    return rows // count, count


def sketch_kernel(
    dims, slot_hbm, wire_hbm, radius_hbm, test_hbm, sketch_ref, gram_ref,
    slot_ref, wire_ref, radius_ref,
    pay, tgeo, columns, halves, partial, landed, gram_plane, gram_line, load_sem,
    pay_send, pay_recv, fwd_send, fwd_recv, geo_send, geo_recv, sum_send, sum_recv,
    gp_send, gp_recv, gl_send, gl_recv,
):
    rows, cols, subs = dims
    plane = cols * subs
    near, halves_count = split_rows(rows)
    line = near * cols
    rank, count = test_hbm.shape
    row, col, sub = lax.axis_index("row"), lax.axis_index("col"), lax.axis_index("sub")

    def plane_peer(o):
        return {
            "col": lax.rem(col + o // subs, cols),
            "sub": lax.rem(sub + o % subs, subs),
        }

    def row_peer(k):
        return {"row": lax.rem(row + k, rows)}

    def line_peer(k):
        return {
            "row": row // near * near + lax.rem(row + k // cols, near),
            "col": lax.rem(col + k % cols, cols),
        }

    def half_peer(o):
        return {"row": lax.rem(row + o * near, rows)}

    loads = [
        pltpu.make_async_copy(slot_hbm, slot_ref, load_sem.at[0]),
        pltpu.make_async_copy(wire_hbm, wire_ref, load_sem.at[1]),
        pltpu.make_async_copy(radius_hbm, radius_ref, load_sem.at[2]),
        pltpu.make_async_copy(test_hbm, pay.at[0, 0, pl.ds(0, rank)], load_sem.at[3]),
    ]
    for load in loads:
        load.start()
    barrier = pltpu.get_barrier_semaphore()
    for o in range(1, plane):
        pl.semaphore_signal(barrier, inc=1, device_id=plane_peer(o), device_id_type=MESH)
    for k in range(1, rows):
        pl.semaphore_signal(barrier, inc=1, device_id=row_peer(k), device_id_type=MESH)
    across = [k for k in range(1, line) if k // cols and k % cols]
    for k in across:
        pl.semaphore_signal(barrier, inc=1, device_id=line_peer(k), device_id_type=MESH)

    for load in loads[:3]:
        load.wait()
    geo = local_geometry(slot_ref[...], wire_ref[...], radius_ref[...])
    pay[0, 0, rank:, :] = geo
    tgeo[0] = geo
    partial[...] = jnp.zeros_like(partial)
    loads[3].wait()
    pl.semaphore_wait(barrier, plane + rows - 2 + len(across))

    def copy_geo(o):
        return pltpu.make_async_remote_copy(
            src_ref=pay.at[0, 0, pl.ds(rank, GEO_ROWS)], dst_ref=tgeo.at[halves_count - o],
            send_sem=geo_send.at[o], recv_sem=geo_recv.at[halves_count - o],
            device_id=half_peer(o), device_id_type=MESH,
        )

    def copy_pay(k):
        return pltpu.make_async_remote_copy(
            src_ref=pay.at[0, 0], dst_ref=pay.at[0, k],
            send_sem=pay_send.at[k], recv_sem=pay_recv.at[k],
            device_id=line_peer(k), device_id_type=MESH,
        )

    def copy_fwd(s, k):
        return pltpu.make_async_remote_copy(
            src_ref=pay.at[0, k], dst_ref=pay.at[subs - s, k],
            send_sem=fwd_send.at[s, k], recv_sem=fwd_recv.at[subs - s, k],
            device_id={"sub": lax.rem(sub + s, subs)}, device_id_type=MESH,
        )

    def copy_sum(o):
        return pltpu.make_async_remote_copy(
            src_ref=partial.at[o], dst_ref=landed.at[o],
            send_sem=sum_send.at[o], recv_sem=sum_recv.at[o],
            device_id=half_peer(o), device_id_type=MESH,
        )

    for o in range(1, halves_count):
        copy_geo(o).start()
    for k in range(1, line):
        copy_pay(k).start()
    for s in range(1, subs):
        copy_fwd(s, 0).start()

    def prepare(s, k):
        columns[s, k] = jnp.concatenate(
            [pay[s, k, rank:, :]] * (128 // GEO_ROWS), axis=0
        ).T
        test = pay[s, k, :rank, :]
        high = test.astype(jnp.bfloat16)
        halves[s, k, :rank, :] = high
        halves[s, k, rank:, :] = (test - high.astype(jnp.float32)).astype(jnp.bfloat16)

    def block(s, k, o):
        for j in range(0, count, 256):
            part = halves[s, k, :, j : j + 256]
            xs, ys = columns[s, k, j : j + 256, 0:1], columns[s, k, j : j + 256, 1:2]
            zs, es = columns[s, k, j : j + 256, 2:3], columns[s, k, j : j + 256, 3:4]
            xt, yt = tgeo[o, 0:1, :], tgeo[o, 1:2, :]
            zt, et = tgeo[o, 2:3, :], tgeo[o, 3:4, :]
            cross = xs * xt + ys * yt
            distance = (es + et) - cross - zs * zt
            kernel = (cross + OFFSET) * lax.rsqrt(distance)
            high = kernel.astype(jnp.bfloat16)
            low = (kernel - high.astype(jnp.float32)).astype(jnp.bfloat16)
            both = jnp.dot(part, high, preferred_element_type=jnp.float32)
            rest = jnp.dot(part[:rank], low, preferred_element_type=jnp.float32)
            partial[o, :, :] += both[:rank] + (both[rank:] + rest)

    @pl.loop(0, line)
    def _(k):
        @pl.when(k > 0)
        def _():
            copy_pay(k).wait_recv()
            for s in range(1, subs):
                copy_fwd(s, k).start()

        @pl.when(k == 0)
        def _():
            for o in range(1, halves_count):
                copy_geo(halves_count - o).wait_recv()

        @pl.loop(0, subs)
        def _(s):
            @pl.when(s > 0)
            def _():
                copy_fwd(subs - s, k).wait_recv()

            prepare(s, k)

            @pl.loop(1, halves_count)
            def _(o):
                block(s, k, o)

    for o in range(1, halves_count):
        copy_sum(o).start()

    @pl.loop(0, line)
    def _(k):
        @pl.loop(0, subs)
        def _(s):
            block(s, k, 0)

    sketch = partial[0]
    for o in range(1, halves_count):
        copy_sum(o).wait_recv()
        sketch = sketch + landed[o]
    sketch_ref[...] = sketch

    gram = lax.dot_general(
        sketch, sketch, (((1,), (1,)), ((), ())),
        precision=lax.Precision.HIGHEST, preferred_element_type=jnp.float32,
    )
    place = col * subs + sub
    gram_plane[place] = jnp.concatenate([gram[: rank // 2], gram[rank // 2 :]], axis=1)

    def copy_gp(o):
        return pltpu.make_async_remote_copy(
            src_ref=gram_plane.at[place], dst_ref=gram_plane.at[place],
            send_sem=gp_send.at[o], recv_sem=gp_recv.at[o],
            device_id=plane_peer(o), device_id_type=MESH,
        )

    def copy_gl(k):
        return pltpu.make_async_remote_copy(
            src_ref=gram_line.at[row], dst_ref=gram_line.at[row],
            send_sem=gl_send.at[k], recv_sem=gl_recv.at[k],
            device_id=row_peer(k), device_id_type=MESH,
        )

    for o in reversed(range(1, plane)):
        copy_gp(o).start()
    for o in range(1, plane):
        copy_gp(o).wait_recv()
    total = gram_plane[0]
    for o in range(1, plane):
        total = total + gram_plane[o]
    gram_line[row] = total
    for k in range(1, rows):
        copy_gl(k).start()
    for o in range(1, plane):
        copy_gp(o).wait_send()
    for o in range(1, halves_count):
        copy_geo(o).wait_send()
        copy_sum(o).wait_send()
    for k in range(1, line):
        copy_pay(k).wait_send()
    for s in range(1, subs):
        for k in range(line):
            copy_fwd(s, k).wait_send()
    for k in range(1, rows):
        copy_gl(k).wait_recv()
    total = gram_line[0]
    for k in range(1, rows):
        total = total + gram_line[k]
    gram_ref[...] = total
    for k in range(1, rows):
        copy_gl(k).wait_send()


def factor_kernel(scale, sketch_ref, gram_ref, basis_ref, factor_ref):
    rank = gram_ref.shape[1] // 2
    tiles = rank // 8
    eye = (
        lax.broadcasted_iota(jnp.int32, (rank, rank), 0)
        == lax.broadcasted_iota(jnp.int32, (rank, rank), 1)
    ).astype(jnp.float32)
    gram = jnp.concatenate([gram_ref[:, :rank], gram_ref[:, rank:]], axis=0)
    wide = jnp.concatenate([gram, eye], axis=1)
    parts = [wide[8 * t : 8 * t + 8] for t in range(tiles)]
    for own in range(tiles):
        base = 8 * own
        lines = [jnp.broadcast_to(parts[own][a : a + 1], (8, 2 * rank)) for a in range(8)]
        inner = {
            (a, b): jnp.broadcast_to(lines[a][:, base + b : base + b + 1], (8, 2 * rank))
            for a in range(8)
            for b in range(a, 8)
        }
        ratio = {}
        for a in range(8):
            inverse = 1.0 / inner[a, a]
            for b in range(a + 1, 8):
                ratio[a, b] = inner[a, b] * inverse
                for c in range(b, 8):
                    inner[b, c] = inner[b, c] - ratio[a, b] * inner[a, c]
                lines[b] = lines[b] - ratio[a, b] * lines[a]
            ratio[a, a] = inverse
        scaled = [lines[a] * ratio[a, a] for a in range(8)]
        for t in range(own + 1, tiles):
            heads = [
                jnp.broadcast_to(parts[t][:, base + a : base + a + 1], (8, 2 * rank))
                for a in range(8)
            ]
            for a in range(8):
                for b in range(a + 1, 8):
                    heads[b] = heads[b] - ratio[a, b] * heads[a]
            terms = [heads[a] * scaled[a] for a in range(8)]
            while len(terms) > 1:
                terms = [terms[i] + terms[i + 1] for i in range(0, len(terms), 2)]
            parts[t] = parts[t] - terms[0]
        parts[own] = jnp.concatenate([lines[a][a : a + 1] for a in range(8)], axis=0)
    wide = jnp.concatenate(parts, axis=0)
    pivots = jnp.sum(wide[:, :rank] * eye, axis=1, keepdims=True)
    wide = wide * lax.rsqrt(pivots)
    upper = (
        lax.broadcasted_iota(jnp.int32, (rank, rank), 0)
        <= lax.broadcasted_iota(jnp.int32, (rank, rank), 1)
    )
    factor_ref[...] = jnp.where(upper, wide[:, :rank], 0.0) * (FOLDED / scale)
    basis_ref[...] = jnp.dot(
        wide[:, rank:] * scale, sketch_ref[...],
        precision=lax.Precision.HIGHEST, preferred_element_type=jnp.float32,
    )


def per_device(filament_slot, wire_radius, strand_radius, test_matrix):
    dims = tuple(lax.axis_size(name) for name in ("row", "col", "sub"))
    rows, cols, subs = dims
    plane = cols * subs
    near, halves_count = split_rows(rows)
    line = near * cols
    rank, count = test_matrix.shape
    vmem = pl.BlockSpec(memory_space=pltpu.VMEM)
    hbm = pl.BlockSpec(memory_space=pltpu.HBM)
    f32 = jnp.float32
    dma = pltpu.SemaphoreType.DMA
    keep = pltpu.with_memory_space_constraint
    sketch, gram = pl.pallas_call(
        functools.partial(sketch_kernel, dims),
        out_shape=(
            jax.ShapeDtypeStruct((rank, count), f32),
            jax.ShapeDtypeStruct((rank // 2, 2 * rank), f32),
        ),
        in_specs=[hbm] * 4,
        out_specs=(vmem, vmem),
        scratch_shapes=[
            pltpu.VMEM((1, count), jnp.int32),
            pltpu.VMEM((1, count), f32),
            pltpu.VMEM((1, strand_radius.shape[0]), f32),
            pltpu.VMEM((subs, line, rank + GEO_ROWS, count), f32),
            pltpu.VMEM((halves_count, GEO_ROWS, count), f32),
            pltpu.VMEM((subs, line, count, 128), f32),
            pltpu.VMEM((subs, line, 2 * rank, count), jnp.bfloat16),
            pltpu.VMEM((halves_count, rank, count), f32),
            pltpu.VMEM((halves_count, rank, count), f32),
            pltpu.VMEM((plane, rank // 2, 2 * rank), f32),
            pltpu.VMEM((rows, rank // 2, 2 * rank), f32),
            dma((4,)),
            dma((line,)), dma((line,)), dma((subs, line)), dma((subs, line)),
            dma((halves_count,)), dma((halves_count,)), dma((halves_count,)), dma((halves_count,)),
            dma((plane,)), dma((plane,)), dma((rows,)), dma((rows,)),
        ],
        compiler_params=pltpu.CompilerParams(
            collective_id=0, has_side_effects=True, vmem_limit_bytes=48 * 1024 * 1024
        ),
    )(
        keep(filament_slot.reshape(1, count), pltpu.HBM),
        keep(wire_radius.reshape(1, count), pltpu.HBM),
        keep(strand_radius.reshape(1, -1), pltpu.HBM),
        keep(test_matrix, pltpu.HBM),
    )
    scale = math.sqrt(count * rows * plane)
    return pl.pallas_call(
        functools.partial(factor_kernel, scale),
        out_shape=(
            jax.ShapeDtypeStruct((rank, count), f32),
            jax.ShapeDtypeStruct((rank, rank), f32),
        ),
        in_specs=[vmem] * 2,
        out_specs=(vmem, vmem),
        compiler_params=pltpu.CompilerParams(vmem_limit_bytes=16 * 1024 * 1024),
    )(sketch, gram)


def solution(mesh):
    return jax.shard_map(
        per_device,
        mesh=mesh,
        in_specs=(
            P(("grp", "row", "col", "sub")),
            P(("grp", "row", "col", "sub")),
            P("grp"),
            P(None, ("grp", "row", "col", "sub")),
        ),
        out_specs=(P(None, ("grp", "row", "col", "sub")), P("grp", None)),
        check_vma=False,
    )
```
